32 devices in a mesh: member: 2 (over x), wide: 16 (over z, y, core).
Axes of the slice: x: 2, y: 2, z: 4, core: 2. Of those that a mesh axis runs over, the one named last changes fastest.
Arguments:
- stream_now: float32 [4, 256, 4096], P('member', 'wide'), parts along dimension 0, may hold values from -6 to 6
- vorticity: float32 [4, 256, 4096], P('member', 'wide'), parts along dimension 0, may hold values from -0.62 to 0.62
Outputs:
- vorticity_next: float32 [4, 256, 4096], P('member', 'wide'), parts along dimension 0
- stream_next: float32 [4, 256, 4096], P('member', 'wide'), parts along dimension 0
The draws below stay inside these ranges and needn't reach their ends.
There are 2 independent parts, one for each index of `member`. The reference program is written for one: setup_inputs(seed, part) draws one part's arguments, and reference() takes and returns one part's arrays. A program takes and returns all parts, laid end to end along the dimension named above; each array names one. Nothing has to cross between parts.
All inputs are finite; a program needn't handle non-finite values.
Results may differ from the reference program's by a relative error of at most 0.00002.
Values sent between devices are 32-bit elements; how exact they have to be, the bound alone decides.
A program may use at most 128 MiB of HBM per device.

```python
import jax
import jax.numpy as jnp

COLS = 4096
LEVELS = 5
SWEEPS = 2
COARSE_SWEEPS = 8
NY = 256


def draw_vorticity(key, part):
    rough_key, phase_key = jax.random.split(jax.random.fold_in(key, 11))
    full_turn = 6.283185307179586
    phases = jax.random.uniform(phase_key, (2, 2), jnp.float32, 0.0, full_turn)
    row_frac = (jnp.arange(NY, dtype=jnp.float32) / NY)[None, :, None]
    col_frac = (jnp.arange(COLS, dtype=jnp.float32) / COLS)[None, None, :]
    wave = jnp.sin(full_turn * row_frac + phases[:, 0, None, None]) * jnp.cos(2.0 * full_turn * col_frac + phases[:, 1, None, None])
    rough = 0.1 * jnp.clip(jax.random.normal(rough_key, (2, NY, COLS), jnp.float32), -6.0, 6.0)
    smooth = 0.01 * wave
    return rough + smooth


def block_levels(rng, shape, cuts, low, largest):
    factor_of, own = 1.0, jax.random.fold_in(rng, 6)
    for axis_at, shards_of in cuts:
        steps = jnp.exp(jax.random.uniform(jax.random.fold_in(own, axis_at), (shards_of,), jnp.float32, low / len(cuts), largest / len(cuts)))
        factor_of = factor_of * jnp.repeat(steps, shape[axis_at] // shards_of).reshape([-1 if axis == axis_at else 1 for axis in range(len(shape))])
    return factor_of


def gaussian(stream_key, extent, scale, most, shards=(), kind=jnp.bfloat16):
    values = jax.random.normal(stream_key, extent, jnp.float32) * scale
    if len(shards) > 0:
        values = block_levels(stream_key, extent, shards, -0.22, 0.18) * values
    return jnp.clip(values, min=-most, max=most).astype(kind)


def setup_inputs(seed: int = 0, part: int = 0) -> dict:
    key_list = jax.random.split(jax.random.key(seed), 3)
    own_keys = jax.random.split(jax.random.fold_in(key_list[2], part), 3)
    return {
        "stream_now": gaussian(own_keys[0], (2, NY, COLS), 1.0, 6.0, ((1, 16),), jnp.float32),
        "vorticity": draw_vorticity(jax.random.fold_in(jax.random.fold_in(key_list[2], part), 71), part),
    }


relax_weight = 0.8
coupling_upper = 0.02
coupling_lower = 0.04
time_step = 0.5
beta_slope = 0.05
bottom_drag = 0.02


def coupling():
    return jnp.array([coupling_upper, coupling_lower], jnp.float32)[:, None, None]


def diagonal(spacing):
    return 4.0 / (spacing * spacing) + coupling()


def pad_rows(iterate):
    return jnp.pad(iterate, ((0, 0), (1, 1), (0, 0)))


def neighbours(padded):
    interior = padded[:, 1:-1, :]
    return padded[:, 2:, :] + padded[:, :-2, :] + jnp.roll(interior, 1, axis=2) + jnp.roll(interior, -1, axis=2)


def apply_operator(padded, spacing):
    interior = padded[:, 1:-1, :]
    return (4.0 * interior - neighbours(padded)) / (spacing * spacing) + coupling() * (interior - interior[::-1])


def jacobi(padded, source, spacing):
    return padded[:, 1:-1, :] + relax_weight * (source - apply_operator(padded, spacing)) / diagonal(spacing)


def shifted(padded, row_step, col_step):
    row_count = padded.shape[1] - 2
    return jnp.roll(padded[:, 1 + row_step:1 + row_step + row_count, :], -col_step, axis=2)


def arakawa(stream_padded, vorticity_padded):
    def stream_at(row_step, col_step):
        return shifted(stream_padded, row_step, col_step)

    def vorticity_at(row_step, col_step):
        return shifted(vorticity_padded, row_step, col_step)

    first_form = (stream_at(0, 1) - stream_at(0, -1)) * (vorticity_at(1, 0) - vorticity_at(-1, 0)) - (stream_at(1, 0) - stream_at(-1, 0)) * (vorticity_at(0, 1) - vorticity_at(0, -1))
    second_form = stream_at(0, 1) * (vorticity_at(1, 1) - vorticity_at(-1, 1)) - stream_at(0, -1) * (vorticity_at(1, -1) - vorticity_at(-1, -1)) - stream_at(1, 0) * (vorticity_at(1, 1) - vorticity_at(1, -1)) + stream_at(-1, 0) * (vorticity_at(-1, 1) - vorticity_at(-1, -1))
    third_form = vorticity_at(1, 0) * (stream_at(1, 1) - stream_at(1, -1)) - vorticity_at(-1, 0) * (stream_at(-1, 1) - stream_at(-1, -1)) - vorticity_at(0, 1) * (stream_at(1, 1) - stream_at(-1, 1)) + vorticity_at(0, -1) * (stream_at(1, -1) - stream_at(-1, -1))
    return (first_form + second_form + third_form) / 12.0


def advance(stream_padded, vorticity_padded, stream_now, vorticity):
    jacobian = arakawa(stream_padded, vorticity_padded)
    zonal_slope = (jnp.roll(stream_now, -1, axis=2) - jnp.roll(stream_now, 1, axis=2)) * 0.5
    drag_term = jnp.array([0.0, bottom_drag], jnp.float32)[:, None, None] * (neighbours(stream_padded) - 4.0 * stream_now)
    return vorticity - time_step * (jacobian + beta_slope * zonal_slope + drag_term)


def restrict(residual):
    return 0.25 * (((residual[:, 0::2, 0::2] + residual[:, 1::2, 0::2]) + residual[:, 0::2, 1::2]) + residual[:, 1::2, 1::2])


def prolong(correction):
    layers, row_count, col_count = correction.shape
    spread = jnp.broadcast_to(correction[:, :, None, :, None], (layers, row_count, 2, col_count, 2))
    return spread.reshape(layers, 2 * row_count, 2 * col_count)


def relax_sweeps(iterate, source, spacing, sweep_count, zero_start):
    for sweep_index in range(sweep_count):
        if zero_start and sweep_index == 0:
            iterate = relax_weight * source / diagonal(spacing)
        else:
            iterate = jacobi(pad_rows(iterate), source, spacing)
    return iterate


def vcycle(grid_level, iterate, source, zero_start):
    spacing = 2.0 ** grid_level
    if grid_level == LEVELS - 1:
        return relax_sweeps(source, source, spacing, COARSE_SWEEPS, True)
    iterate = relax_sweeps(iterate, source, spacing, SWEEPS, zero_start)
    residual = source - apply_operator(pad_rows(iterate), spacing)
    coarse_source = restrict(residual)
    correction = vcycle(grid_level + 1, coarse_source, coarse_source, True)
    iterate = iterate + prolong(correction)
    return relax_sweeps(iterate, source, spacing, SWEEPS, False)


def reference(stream_now, vorticity):
    vorticity_next = advance(pad_rows(stream_now), pad_rows(vorticity), stream_now, vorticity)
    stream_next = vcycle(0, stream_now, -vorticity_next, False)
    return vorticity_next, stream_next
```

```python
import functools

import jax
import jax.numpy as jnp
from jax import lax
from jax.experimental import pallas as pl
from jax.experimental.pallas import tpu as pltpu
from jax.sharding import PartitionSpec as P

MESH = pl.DeviceIdType.MESH
WEIGHT = 0.8
F = (0.02, 0.04)
DT = 0.5
BETA = 0.05
DRAG = 0.02

ROWS = 16
WIDTH = (4, 2, 1, 1, 1)
STEP = (1, 1, 1, 2, 4)
HALO = (4, 4, 5, 20, 9)
OWN = (16, 8, 4, 2, 1)
EXT = tuple(o + 2 * h for o, h in zip(OWN, HALO))
REACH = 10


def rows_loop(lo, hi, body, unroll=4):
    count = hi - lo
    if count <= unroll:
        for r in range(lo, hi):
            body(r)
        return
    trips = count // unroll

    def trip(i, carry):
        for j in range(unroll):
            body(lo + i * unroll + j)
        return carry

    lax.fori_loop(0, trips, trip, 0)
    for r in range(lo + trips * unroll, hi):
        body(r)


def kernel(n, pq_ref, qn_ref, sn_ref, pq, b0, a0, c0, b1, a1, c1, b2, a2, c2, b3, a3, c3, b4, a4, c4, send, recv):
    me = lax.axis_index("wide")
    sub = lax.broadcasted_iota(jnp.int32, (8, 128), 0)
    first = [sub < s for s in (1, 1, 1, 2, 4)]
    last = [sub >= 8 - s for s in (1, 1, 1, 2, 4)]
    odd1 = (sub & 1) != 0
    odd2 = (sub & 2) != 0
    zero = jnp.zeros((8, 128), jnp.float32)

    def east(v, level):
        s = STEP[level]
        z = pltpu.roll(v[0], 8 - s, 0)
        return v[1:] + [jnp.where(last[level], pltpu.roll(z, 127, 1), z)]

    def west(v, level):
        s = STEP[level]
        z = pltpu.roll(v[-1], s, 0)
        return [jnp.where(first[level], pltpu.roll(z, 1, 1), z)] + v[:-1]

    def mask(r, level):
        g = me * OWN[level] + r - HALO[level]
        return jnp.where(jnp.logical_and(g >= 0, g < n * OWN[level]), 1.0, 0.0).astype(jnp.float32)

    def load(ref, r, level):
        return [[ref[r, k, u] for u in range(WIDTH[level])] for k in range(2)]

    def load_p(ref, r, level):
        return [[ref[r, 0, k, u] for u in range(4)] for k in range(2)]

    def around(src, r, level, get):
        up, mid, down = get(src, r + 1, level), get(src, r, level), get(src, r - 1, level)
        nb = []
        for k in range(2):
            e, w = east(mid[k], level), west(mid[k], level)
            nb.append([up[k][u] + down[k][u] + (e[u] + w[u]) for u in range(WIDTH[level])])
        return mid, nb

    def sweep(src, dst, b, lo, hi, level, get=load, out=None, unroll=4):
        h2 = 4.0**level

        def body(r):
            m = mask(r, level)
            mid, nb = around(src, r, level, get)
            for k in range(2):
                c = m * (WEIGHT / (4.0 / h2 + F[k]))
                keep = m * (1.0 - WEIGHT)
                for u in range(WIDTH[level]):
                    new = keep * mid[k][u] + c * (
                        b[r, k, u] + nb[k][u] * (1.0 / h2) + F[k] * mid[1 - k][u]
                    )
                    if out is None:
                        dst[r, k, u] = new
                    else:
                        dst[r - HALO[level], k, u] = new

        rows_loop(lo, hi, body, unroll)

    def from_zero(dst, b, lo, hi, level):
        def body(r):
            m = mask(r, level)
            for k in range(2):
                c = m * (WEIGHT / (4.0 / 4.0**level + F[k]))
                for u in range(WIDTH[level]):
                    dst[r, k, u] = c * b[r, k, u]

        rows_loop(lo, hi, body)

    def residual(v, b, coarse, lo, count, at, level):
        h2 = 4.0**level
        wide = WIDTH[level]

        def body(i):
            total = [[zero] * wide for _ in range(2)]
            for j in range(2):
                r = lo + 2 * i + j
                mid, nb = around(v, r, level, load)
                for k in range(2):
                    for u in range(wide):
                        x = (
                            b[r, k, u]
                            + (nb[k][u] - 4.0 * mid[k][u]) * (1.0 / h2)
                            - F[k] * (mid[k][u] - mid[1 - k][u])
                        )
                        total[k][u] = x if j == 0 else total[k][u] + x
            for k in range(2):
                t = total[k]
                if level < 2:
                    for u in range(wide // 2):
                        coarse[at + i, k, u] = 0.25 * (t[2 * u] + t[2 * u + 1])
                else:
                    s = 1 if level == 2 else 2
                    odd = odd1 if level == 2 else odd2
                    other = jnp.where(odd, pltpu.roll(t[0], s, 0), pltpu.roll(t[0], 8 - s, 0))
                    coarse[at + i, k, 0] = 0.25 * (t[0] + other)

        rows_loop(0, count, body, 2)

    def prolong(v, coarse, lo, hi, level, shift):
        def body(r):
            i = (r + shift) // 2 if isinstance(r, int) else lax.div(r + shift, 2)
            for k in range(2):
                for u in range(WIDTH[level]):
                    cu = u // 2 if level < 2 else u
                    v[r, k, u] = v[r, k, u] + coarse[i, k, cu]

        rows_loop(lo, hi, body)

    def inside(d):
        return jnp.logical_and(me + d >= 0, me + d < n)

    copies = []

    def put(d, src, dst):
        copies.append((d, src, dst))
        return len(copies) - 1

    def copy(i, d, src, dst):
        return pltpu.make_async_remote_copy(
            src_ref=src,
            dst_ref=dst,
            send_sem=send.at[i],
            recv_sem=recv.at[i],
            device_id={"wide": me + d},
            device_id_type=MESH,
        )

    def start(ids):
        for i in ids:
            d, src, dst = copies[i]

            @pl.when(inside(d))
            def _():
                copy(i, d, src, dst).start()

    def arrive(ids):
        for i in ids:
            d, src, dst = copies[i]

            @pl.when(inside(-d))
            def _():
                copy(i, -d, src, dst).wait_recv()

    def depart(ids):
        for i in ids:
            d, src, dst = copies[i]

            @pl.when(inside(d))
            def _():
                copy(i, d, src, dst).wait_send()

    reach = min(REACH, n - 1)
    phase_a = [
        put(1, pq_ref.at[pl.ds(12, 4)], pq.at[pl.ds(0, 4)]),
        put(-1, pq_ref.at[pl.ds(0, 4)], pq.at[pl.ds(20, 4)]),
    ]
    phase_b = [
        put(1, b1.at[pl.ds(8, 4)], b1.at[pl.ds(0, 4)]),
        put(-1, b1.at[pl.ds(4, 4)], b1.at[pl.ds(12, 4)]),
    ]
    phase_c = [
        put(1, b2.at[pl.ds(5, 4)], b2.at[pl.ds(1, 4)]),
        put(-1, b2.at[pl.ds(5, 4)], b2.at[pl.ds(9, 4)]),
        put(2, b2.at[pl.ds(8, 1)], b2.at[pl.ds(0, 1)]),
        put(-2, b2.at[pl.ds(5, 1)], b2.at[pl.ds(13, 1)]),
    ]
    phase_d = []
    for d in range(reach, 0, -1):
        for signed in (d, -d):
            phase_d.append(put(signed, b3.at[pl.ds(20, 2)], b3.at[pl.ds(20 - 2 * signed, 2)]))

    def clear(ref, lo, hi, inner):
        for r in range(lo, hi):
            for index in inner:
                ref[(r, *index)] = zero

    pairs = [(k, u) for k in range(2) for u in range(4)]

    @pl.when(me == 0)
    def _():
        clear(pq, 0, 4, [(f, k, u) for f in range(2) for k, u in pairs])

    @pl.when(me == n - 1)
    def _():
        clear(pq, 20, 24, [(f, k, u) for f in range(2) for k, u in pairs])

    clear(b1, 0, 4, [(k, u) for k in range(2) for u in range(2)])
    clear(b1, 12, 16, [(k, u) for k in range(2) for u in range(2)])
    clear(b2, 0, 5, [(0, 0), (1, 0)])
    clear(b2, 9, 14, [(0, 0), (1, 0)])
    clear(b3, 0, 20, [(0, 0), (1, 0)])
    clear(b3, 22, 42, [(0, 0), (1, 0)])

    barrier = pltpu.get_barrier_semaphore()
    for d in range(-reach, reach + 1):
        if d:

            @pl.when(inside(d))
            def _():
                pl.semaphore_signal(barrier, inc=1, device_id={"wide": me + d}, device_id_type=MESH)

    pl.semaphore_wait(barrier, jnp.minimum(me, reach) + jnp.minimum(n - 1 - me, reach))

    start(phase_a)

    def take(r):
        for f in range(2):
            for k, u in pairs:
                pq[r + 4, f, k, u] = pq_ref[r, f, k, u]

    rows_loop(0, 16, take, 2)

    def advance(lo, hi, own):
        def body(r):
            for k in range(2):
                p = [[pq[r + j, 0, k, u] for u in range(4)] for j in (-1, 0, 1)]
                q = [[pq[r + j, 1, k, u] for u in range(4)] for j in (-1, 0, 1)]
                pe, pw = [east(x, 0) for x in p], [west(x, 0) for x in p]
                qe, qw = [east(x, 0) for x in q], [west(x, 0) for x in q]
                for u in range(4):
                    ps, pc, pn = (x[u] for x in p)
                    qs, qc, qnn = (x[u] for x in q)
                    pse, pce, pne = (x[u] for x in pe)
                    psw, pcw, pnw = (x[u] for x in pw)
                    qse, qce, qne = (x[u] for x in qe)
                    qsw, qcw, qnw = (x[u] for x in qw)
                    ns = qnn - qs
                    ew = qce - qcw
                    jac = (
                        pce * (ns + (qne - qse))
                        - pcw * (ns + (qnw - qsw))
                        - pn * (ew + (qne - qnw))
                        + ps * (ew + (qse - qsw))
                        + pne * (qnn - qce)
                        - pnw * (qnn - qcw)
                        - pse * (qs - qce)
                        + psw * (qs - qcw)
                    )
                    change = jac * (DT / 12.0) + (pce - pcw) * (DT * BETA * 0.5)
                    if k == 1:
                        change = change + (DT * DRAG) * ((pn + ps) + (pcw + pce) - 4.0 * pc)
                    b0[r, k, u] = change - qc
                    if own:
                        qn_ref[r - 4, k, u] = qc - change

        rows_loop(lo, hi, body, 1)

    advance(5, 19, True)
    arrive(phase_a)
    advance(1, 4, False)
    advance(4, 5, True)
    advance(19, 20, True)
    advance(20, 23, False)

    sweep(pq, a0, b0, 1, 23, 0, load_p, unroll=2)
    sweep(a0, c0, b0, 2, 22, 0, unroll=2)
    residual(c0, b0, b1, 4, 8, 4, 0)

    start(phase_b)
    arrive(phase_b)
    from_zero(a1, b1, 0, 16, 1)
    sweep(a1, c1, b1, 1, 15, 1)
    residual(c1, b1, b2, 4, 4, 5, 1)

    start(phase_c)
    arrive(phase_c)
    from_zero(a2, b2, 0, 14, 2)
    sweep(a2, c2, b2, 1, 13, 2)
    residual(c2, b2, b3, 5, 2, 20, 2)

    start(phase_d)
    arrive(phase_d)
    from_zero(a3, b3, 0, 42, 3)
    sweep(a3, c3, b3, 1, 41, 3)
    residual(c3, b3, b4, 2, 19, 0, 3)

    from_zero(a4, b4, 0, 19, 4)
    x, y = a4, c4
    for j in range(1, 8):
        sweep(x, y, b4, j, 19 - j, 4)
        x, y = y, x

    prolong(c3, x, 16, 26, 3, -2)
    sweep(c3, a3, b3, 17, 25, 3)
    sweep(a3, c3, b3, 18, 24, 3)

    prolong(c2, c3, 1, 13, 2, 35)
    sweep(c2, a2, b2, 2, 12, 2)
    sweep(a2, c2, b2, 3, 11, 2)

    prolong(c1, c2, 1, 15, 1, 6)
    sweep(c1, a1, b1, 2, 14, 1)
    sweep(a1, c1, b1, 3, 13, 1)

    prolong(c0, c1, 2, 22, 0, 4)
    sweep(c0, a0, b0, 3, 21, 0, unroll=2)
    sweep(a0, sn_ref, b0, 4, 20, 0, out=True, unroll=2)

    depart(range(len(copies)))


def spread(x):
    layers, rows, cols = x.shape
    return x.reshape(layers, rows, 128, 8, 4).transpose(1, 0, 4, 3, 2)


def gather(x):
    rows, layers = x.shape[:2]
    return x.transpose(1, 0, 4, 3, 2).reshape(layers, rows, 4096)


def shards(stream_now, vorticity):
    n = lax.axis_size("wide")
    pq = jnp.stack([spread(stream_now), spread(vorticity)], axis=1)
    vmem = pl.BlockSpec(memory_space=pltpu.VMEM)
    shape = jax.ShapeDtypeStruct((ROWS, 2, 4, 8, 128), jnp.float32)
    scratch = [pltpu.VMEM((EXT[0], 2, 2, 4, 8, 128), jnp.float32)]
    for level in range(5):
        scratch += [pltpu.VMEM((EXT[level], 2, WIDTH[level], 8, 128), jnp.float32)] * 3
    count = 8 + 2 * min(REACH, n - 1)
    qn, sn = pl.pallas_call(
        functools.partial(kernel, n),
        out_shape=(shape, shape),
        in_specs=[vmem],
        out_specs=(vmem, vmem),
        scratch_shapes=scratch
        + [pltpu.SemaphoreType.DMA((count,)), pltpu.SemaphoreType.DMA((count,))],
        compiler_params=pltpu.CompilerParams(
            collective_id=0, has_side_effects=True, vmem_limit_bytes=40 * 1024 * 1024
        ),
    )(pq)
    return gather(qn), gather(sn)


def solution(mesh):
    return jax.shard_map(
        shards,
        mesh=mesh,
        in_specs=(P("member", "wide", None), P("member", "wide", None)),
        out_specs=(P("member", "wide", None), P("member", "wide", None)),
        check_vma=False,
    )
```

```python
import functools

import jax
import jax.numpy as jnp
from jax import lax
from jax.experimental import pallas as pl
from jax.experimental.pallas import tpu as pltpu
from jax.sharding import PartitionSpec as P

MESH = pl.DeviceIdType.MESH
WEIGHT = 0.8
F = (0.02, 0.04)
DT = 0.5
BETA = 0.05
DRAG = 0.02

ROWS = 16
WIDTH = (4, 2, 1, 1, 1)
STEP = (1, 1, 1, 2, 4)
HALO = (4, 4, 5, 20, 9)
OWN = (16, 8, 4, 2, 1)
EXT = tuple(o + 2 * h for o, h in zip(OWN, HALO))
REACH = 10


def rows_loop(lo, hi, body, unroll=4):
    count = hi - lo
    if count <= unroll:
        for r in range(lo, hi):
            body(r)
        return
    trips = count // unroll

    def trip(i, carry):
        for j in range(unroll):
            body(lo + i * unroll + j)
        return carry

    lax.fori_loop(0, trips, trip, 0)
    for r in range(lo + trips * unroll, hi):
        body(r)


def to_chunks(load4, store, xs, ts):
    for a in range(32):
        xs[pl.ds(4 * a, 4), :] = load4(a)
    ts[...] = xs[...].T
    lane = lax.broadcasted_iota(jnp.int32, (8, 128), 1) & 3
    for u in range(4):
        part = [ts[pl.ds(32 * c + u, 8, stride=4), :] for c in range(4)]
        for q in range(4):
            out = part[q]
            for c in range(4):
                if c != q:
                    out = jnp.where(lane == c, pltpu.roll(part[c], (c - q) % 128, 1), out)
            store(q, u, out)


def from_chunks(load, store4, xs, ts):
    lane = lax.broadcasted_iota(jnp.int32, (8, 128), 1) & 3
    for u in range(4):
        part = [load(q, u) for q in range(4)]
        for c in range(4):
            out = part[c]
            for q in range(4):
                if q != c:
                    out = jnp.where(lane == q, pltpu.roll(part[q], (q - c) % 128, 1), out)
            ts[pl.ds(32 * c + u, 8, stride=4), :] = out
    xs[...] = ts[...].T
    for a in range(32):
        store4(a, xs[pl.ds(4 * a, 4), :])


def kernel(n, p_in, q_in, qn_out, sn_out, xs, ts, qn_ref, sn_ref, pq, b0, a0, c0, b1, a1, c1, b2, a2, c2, b3, a3, c3, b4, a4, c4, send, recv):
    me = lax.axis_index("wide")
    sub = lax.broadcasted_iota(jnp.int32, (8, 128), 0)
    first = [sub < s for s in (1, 1, 1, 2, 4)]
    last = [sub >= 8 - s for s in (1, 1, 1, 2, 4)]
    odd1 = (sub & 1) != 0
    odd2 = (sub & 2) != 0
    zero = jnp.zeros((8, 128), jnp.float32)

    def east(v, level):
        s = STEP[level]
        z = pltpu.roll(v[0], 8 - s, 0)
        return v[1:] + [jnp.where(last[level], pltpu.roll(z, 127, 1), z)]

    def west(v, level):
        s = STEP[level]
        z = pltpu.roll(v[-1], s, 0)
        return [jnp.where(first[level], pltpu.roll(z, 1, 1), z)] + v[:-1]

    def mask(r, level):
        g = me * OWN[level] + r - HALO[level]
        return jnp.where(jnp.logical_and(g >= 0, g < n * OWN[level]), 1.0, 0.0).astype(jnp.float32)

    def load(ref, r, level):
        return [[ref[r, k, u] for u in range(WIDTH[level])] for k in range(2)]

    def load_p(ref, r, level):
        return [[ref[r, 0, k, u] for u in range(4)] for k in range(2)]

    def around(src, r, level, get):
        up, mid, down = get(src, r + 1, level), get(src, r, level), get(src, r - 1, level)
        nb = []
        for k in range(2):
            e, w = east(mid[k], level), west(mid[k], level)
            nb.append([up[k][u] + down[k][u] + (e[u] + w[u]) for u in range(WIDTH[level])])
        return mid, nb

    def sweep(src, dst, b, lo, hi, level, get=load, out=None, unroll=4):
        h2 = 4.0**level

        def body(r):
            m = mask(r, level)
            mid, nb = around(src, r, level, get)
            for k in range(2):
                c = m * (WEIGHT / (4.0 / h2 + F[k]))
                keep = m * (1.0 - WEIGHT)
                for u in range(WIDTH[level]):
                    new = keep * mid[k][u] + c * (
                        b[r, k, u] + nb[k][u] * (1.0 / h2) + F[k] * mid[1 - k][u]
                    )
                    if out is None:
                        dst[r, k, u] = new
                    else:
                        dst[r - HALO[level], k, u] = new

        rows_loop(lo, hi, body, unroll)

    def from_zero(dst, b, lo, hi, level):
        def body(r):
            m = mask(r, level)
            for k in range(2):
                c = m * (WEIGHT / (4.0 / 4.0**level + F[k]))
                for u in range(WIDTH[level]):
                    dst[r, k, u] = c * b[r, k, u]

        rows_loop(lo, hi, body)

    def residual(v, b, coarse, lo, count, at, level):
        h2 = 4.0**level
        wide = WIDTH[level]

        def body(i):
            total = [[zero] * wide for _ in range(2)]
            for j in range(2):
                r = lo + 2 * i + j
                mid, nb = around(v, r, level, load)
                for k in range(2):
                    for u in range(wide):
                        x = (
                            b[r, k, u]
                            + (nb[k][u] - 4.0 * mid[k][u]) * (1.0 / h2)
                            - F[k] * (mid[k][u] - mid[1 - k][u])
                        )
                        total[k][u] = x if j == 0 else total[k][u] + x
            for k in range(2):
                t = total[k]
                if level < 2:
                    for u in range(wide // 2):
                        coarse[at + i, k, u] = 0.25 * (t[2 * u] + t[2 * u + 1])
                else:
                    s = 1 if level == 2 else 2
                    odd = odd1 if level == 2 else odd2
                    other = jnp.where(odd, pltpu.roll(t[0], s, 0), pltpu.roll(t[0], 8 - s, 0))
                    coarse[at + i, k, 0] = 0.25 * (t[0] + other)

        rows_loop(0, count, body, 2 if level == 0 else 5)

    def prolong(v, coarse, lo, hi, level, shift):
        def body(r):
            i = (r + shift) // 2 if isinstance(r, int) else lax.div(r + shift, 2)
            for k in range(2):
                for u in range(WIDTH[level]):
                    cu = u // 2 if level < 2 else u
                    v[r, k, u] = v[r, k, u] + coarse[i, k, cu]

        rows_loop(lo, hi, body)

    def inside(d):
        return jnp.logical_and(me + d >= 0, me + d < n)

    copies = []

    def put(d, src, dst):
        copies.append((d, src, dst))
        return len(copies) - 1

    def copy(i, d, src, dst):
        return pltpu.make_async_remote_copy(
            src_ref=src,
            dst_ref=dst,
            send_sem=send.at[i],
            recv_sem=recv.at[i],
            device_id={"wide": me + d},
            device_id_type=MESH,
        )

    def start(ids):
        for i in ids:
            d, src, dst = copies[i]

            @pl.when(inside(d))
            def _():
                copy(i, d, src, dst).start()

    def arrive(ids):
        for i in ids:
            d, src, dst = copies[i]

            @pl.when(inside(-d))
            def _():
                copy(i, -d, src, dst).wait_recv()

    def depart(ids):
        for i in ids:
            d, src, dst = copies[i]

            @pl.when(inside(d))
            def _():
                copy(i, d, src, dst).wait_send()

    reach = min(REACH, n - 1)
    phase_a = [
        put(1, pq.at[pl.ds(16, 4)], pq.at[pl.ds(0, 4)]),
        put(-1, pq.at[pl.ds(4, 4)], pq.at[pl.ds(20, 4)]),
    ]
    phase_b = [
        put(1, b1.at[pl.ds(8, 4)], b1.at[pl.ds(0, 4)]),
        put(-1, b1.at[pl.ds(4, 4)], b1.at[pl.ds(12, 4)]),
    ]
    phase_c = [
        put(1, b2.at[pl.ds(5, 4)], b2.at[pl.ds(1, 4)]),
        put(-1, b2.at[pl.ds(5, 4)], b2.at[pl.ds(9, 4)]),
        put(2, b2.at[pl.ds(8, 1)], b2.at[pl.ds(0, 1)]),
        put(-2, b2.at[pl.ds(5, 1)], b2.at[pl.ds(13, 1)]),
    ]
    phase_d = []
    for d in range(reach, 0, -1):
        for signed in (d, -d):
            phase_d.append(put(signed, b3.at[pl.ds(20, 2)], b3.at[pl.ds(20 - 2 * signed, 2)]))

    def clear(ref, lo, hi, inner):
        for r in range(lo, hi):
            for index in inner:
                ref[(r, *index)] = zero

    pairs = [(k, u) for k in range(2) for u in range(4)]

    @pl.when(me == 0)
    def _():
        clear(pq, 0, 4, [(f, k, u) for f in range(2) for k, u in pairs])

    @pl.when(me == n - 1)
    def _():
        clear(pq, 20, 24, [(f, k, u) for f in range(2) for k, u in pairs])

    clear(b1, 0, 4, [(k, u) for k in range(2) for u in range(2)])
    clear(b1, 12, 16, [(k, u) for k in range(2) for u in range(2)])
    clear(b2, 0, 5, [(0, 0), (1, 0)])
    clear(b2, 9, 14, [(0, 0), (1, 0)])
    clear(b3, 0, 20, [(0, 0), (1, 0)])
    clear(b3, 22, 42, [(0, 0), (1, 0)])

    barrier = pltpu.get_barrier_semaphore()
    for d in range(-reach, reach + 1):
        if d:

            @pl.when(inside(d))
            def _():
                pl.semaphore_signal(barrier, inc=1, device_id={"wide": me + d}, device_id_type=MESH)

    def take(j):
        def layer(k, carry):
            for f, ref in enumerate((p_in, q_in)):

                def load4(a):
                    return ref[k, pl.ds(4 * j, 4), pl.ds(128 * a, 128)]

                def store(q, u, x):
                    pq[4 + 4 * j + q, f, k, u] = x

                to_chunks(load4, store, xs.at[f], ts.at[f])
            return carry

        lax.fori_loop(0, 2, layer, 0)

    def give(ref, out):
        def layer(k, carry):
            for j in range(4):

                def load1(q, u):
                    return ref[4 * j + q, k, u]

                def store4(a, x):
                    out[k, pl.ds(4 * j, 4), pl.ds(128 * a, 128)] = x

                from_chunks(load1, store4, xs.at[j % 2], ts.at[j % 2])
            return carry

        lax.fori_loop(0, 2, layer, 0)

    take(0)
    take(3)
    pl.semaphore_wait(barrier, jnp.minimum(me, reach) + jnp.minimum(n - 1 - me, reach))
    start(phase_a)
    take(1)
    take(2)

    def advance(lo, hi, own):
        def body(r):
            for k in range(2):
                p = [[pq[r + j, 0, k, u] for u in range(4)] for j in (-1, 0, 1)]
                q = [[pq[r + j, 1, k, u] for u in range(4)] for j in (-1, 0, 1)]
                pe, pw = [east(x, 0) for x in p], [west(x, 0) for x in p]
                qe, qw = [east(x, 0) for x in q], [west(x, 0) for x in q]
                for u in range(4):
                    ps, pc, pn = (x[u] for x in p)
                    qs, qc, qnn = (x[u] for x in q)
                    pse, pce, pne = (x[u] for x in pe)
                    psw, pcw, pnw = (x[u] for x in pw)
                    qse, qce, qne = (x[u] for x in qe)
                    qsw, qcw, qnw = (x[u] for x in qw)
                    ns = qnn - qs
                    ew = qce - qcw
                    jac = (
                        pce * (ns + (qne - qse))
                        - pcw * (ns + (qnw - qsw))
                        - pn * (ew + (qne - qnw))
                        + ps * (ew + (qse - qsw))
                        + pne * (qnn - qce)
                        - pnw * (qnn - qcw)
                        - pse * (qs - qce)
                        + psw * (qs - qcw)
                    )
                    change = jac * (DT / 12.0) + (pce - pcw) * (DT * BETA * 0.5)
                    if k == 1:
                        change = change + (DT * DRAG) * ((pn + ps) + (pcw + pce) - 4.0 * pc)
                    b0[r, k, u] = change - qc
                    if own:
                        qn_ref[r - 4, k, u] = qc - change

        rows_loop(lo, hi, body, 1)

    advance(5, 19, True)
    arrive(phase_a)
    advance(1, 4, False)
    advance(4, 5, True)
    advance(19, 20, True)
    advance(20, 23, False)

    sweep(pq, a0, b0, 1, 23, 0, load_p, unroll=2)
    sweep(a0, c0, b0, 2, 22, 0, unroll=2)
    residual(c0, b0, b1, 4, 8, 4, 0)

    start(phase_b)
    give(qn_ref, qn_out)
    arrive(phase_b)
    from_zero(a1, b1, 0, 16, 1)
    sweep(a1, c1, b1, 1, 15, 1, unroll=7)
    residual(c1, b1, b2, 4, 4, 5, 1)

    start(phase_c)
    arrive(phase_c)
    from_zero(a2, b2, 0, 14, 2)
    sweep(a2, c2, b2, 1, 13, 2, unroll=12)
    residual(c2, b2, b3, 5, 2, 20, 2)

    start(phase_d)
    arrive(phase_d)
    from_zero(a3, b3, 0, 42, 3)
    sweep(a3, c3, b3, 1, 41, 3, unroll=10)
    residual(c3, b3, b4, 2, 19, 0, 3)

    from_zero(a4, b4, 0, 19, 4)
    x, y = a4, c4
    for j in range(1, 8):
        sweep(x, y, b4, j, 19 - j, 4, unroll=20)
        x, y = y, x

    prolong(c3, x, 16, 26, 3, -2)
    sweep(c3, a3, b3, 17, 25, 3, unroll=8)
    sweep(a3, c3, b3, 18, 24, 3, unroll=8)

    prolong(c2, c3, 1, 13, 2, 35)
    sweep(c2, a2, b2, 2, 12, 2, unroll=12)
    sweep(a2, c2, b2, 3, 11, 2, unroll=12)

    prolong(c1, c2, 1, 15, 1, 6)
    sweep(c1, a1, b1, 2, 14, 1, unroll=6)
    sweep(a1, c1, b1, 3, 13, 1, unroll=5)

    prolong(c0, c1, 2, 22, 0, 4)
    sweep(c0, a0, b0, 3, 21, 0, unroll=2)
    sweep(a0, sn_ref, b0, 4, 20, 0, out=True, unroll=2)

    give(sn_ref, sn_out)
    depart(range(len(copies)))


def shards(stream_now, vorticity):
    n = lax.axis_size("wide")
    vmem = pl.BlockSpec(memory_space=pltpu.VMEM)
    shape = jax.ShapeDtypeStruct((2, ROWS, 4096), jnp.float32)
    scratch = [pltpu.VMEM((2, 128, 128), jnp.float32)] * 2
    scratch += [pltpu.VMEM((ROWS, 2, 4, 8, 128), jnp.float32)] * 2
    scratch += [pltpu.VMEM((EXT[0], 2, 2, 4, 8, 128), jnp.float32)]
    for level in range(5):
        scratch += [pltpu.VMEM((EXT[level], 2, WIDTH[level], 8, 128), jnp.float32)] * 3
    count = 8 + 2 * min(REACH, n - 1)
    return pl.pallas_call(
        functools.partial(kernel, n),
        out_shape=(shape, shape),
        in_specs=[vmem, vmem],
        out_specs=(vmem, vmem),
        scratch_shapes=scratch
        + [pltpu.SemaphoreType.DMA((count,)), pltpu.SemaphoreType.DMA((count,))],
        compiler_params=pltpu.CompilerParams(
            collective_id=0, has_side_effects=True, vmem_limit_bytes=40 * 1024 * 1024
        ),
    )(stream_now, vorticity)


def solution(mesh):
    return jax.shard_map(
        shards,
        mesh=mesh,
        in_specs=(P("member", "wide", None), P("member", "wide", None)),
        out_specs=(P("member", "wide", None), P("member", "wide", None)),
        check_vma=False,
    )
```

```python
import functools

import jax
import jax.numpy as jnp
from jax import lax
from jax.experimental import pallas as pl
from jax.experimental.pallas import tpu as pltpu
from jax.sharding import PartitionSpec as P

MESH = pl.DeviceIdType.MESH
WEIGHT = 0.8
F = (0.02, 0.04)
DT = 0.5
BETA = 0.05
DRAG = 0.02

ROWS = 16
WIDTH = (4, 2, 1, 1, 1)
STEP = (1, 1, 1, 2, 4)
HALO = (4, 4, 5, 20, 9)
OWN = (16, 8, 4, 2, 1)
EXT = tuple(o + 2 * h for o, h in zip(OWN, HALO))
REACH = 10


def rows_loop(lo, hi, body, unroll=4):
    count = hi - lo
    if count <= unroll:
        for r in range(lo, hi):
            body(r)
        return
    trips = count // unroll

    def trip(i, carry):
        for j in range(unroll):
            body(lo + i * unroll + j)
        return carry

    lax.fori_loop(0, trips, trip, 0)
    for r in range(lo + trips * unroll, hi):
        body(r)


def to_chunks(load4, store, xs, ts):
    for a in range(32):
        xs[pl.ds(4 * a, 4), :] = load4(a)
    ts[...] = xs[...].T
    lane = lax.broadcasted_iota(jnp.int32, (8, 128), 1) & 3
    for u in range(4):
        part = [ts[pl.ds(32 * c + u, 8, stride=4), :] for c in range(4)]
        for q in range(4):
            out = part[q]
            for c in range(4):
                if c != q:
                    out = jnp.where(lane == c, pltpu.roll(part[c], (c - q) % 128, 1), out)
            store(q, u, out)


def from_chunks(load, store4, xs, ts):
    lane = lax.broadcasted_iota(jnp.int32, (8, 128), 1) & 3
    for u in range(4):
        part = [load(q, u) for q in range(4)]
        for c in range(4):
            out = part[c]
            for q in range(4):
                if q != c:
                    out = jnp.where(lane == q, pltpu.roll(part[q], (q - c) % 128, 1), out)
            ts[pl.ds(32 * c + u, 8, stride=4), :] = out
    xs[...] = ts[...].T
    for a in range(32):
        store4(a, xs[pl.ds(4 * a, 4), :])


def kernel(n, p_in, q_in, qn_out, sn_out, xs, ts, qn_ref, sn_ref, pq, b0, a0, c0, b1, a1, c1, b2, a2, c2, b3, a3, c3, b4, a4, c4, g3, send, recv):
    me = lax.axis_index("wide")
    sub = lax.broadcasted_iota(jnp.int32, (8, 128), 0)
    first = [sub < s for s in (1, 1, 1, 2, 4)]
    last = [sub >= 8 - s for s in (1, 1, 1, 2, 4)]
    odd1 = (sub & 1) != 0
    odd2 = (sub & 2) != 0
    zero = jnp.zeros((8, 128), jnp.float32)

    def east(v, level):
        s = STEP[level]
        z = pltpu.roll(v[0], 8 - s, 0)
        return v[1:] + [jnp.where(last[level], pltpu.roll(z, 127, 1), z)]

    def west(v, level):
        s = STEP[level]
        z = pltpu.roll(v[-1], s, 0)
        return [jnp.where(first[level], pltpu.roll(z, 1, 1), z)] + v[:-1]

    def mask(r, level):
        g = me * OWN[level] + r - HALO[level]
        return jnp.where(jnp.logical_and(g >= 0, g < n * OWN[level]), 1.0, 0.0).astype(jnp.float32)

    def load(ref, r, level):
        return [[ref[r, k, u] for u in range(WIDTH[level])] for k in range(2)]

    def load_p(ref, r, level):
        return [[ref[r, 0, k, u] for u in range(4)] for k in range(2)]

    def around(src, r, level, get):
        up, mid, down = get(src, r + 1, level), get(src, r, level), get(src, r - 1, level)
        nb = []
        for k in range(2):
            e, w = east(mid[k], level), west(mid[k], level)
            nb.append([up[k][u] + down[k][u] + (e[u] + w[u]) for u in range(WIDTH[level])])
        return mid, nb

    def sweep(src, dst, b, lo, hi, level, get=load, out=None, unroll=4):
        h2 = 4.0**level

        def body(r):
            m = mask(r, level)
            mid, nb = around(src, r, level, get)
            for k in range(2):
                c = m * (WEIGHT / (4.0 / h2 + F[k]))
                keep = m * (1.0 - WEIGHT)
                for u in range(WIDTH[level]):
                    new = keep * mid[k][u] + c * (
                        b[r, k, u] + nb[k][u] * (1.0 / h2) + F[k] * mid[1 - k][u]
                    )
                    if out is None:
                        dst[r, k, u] = new
                    else:
                        dst[r - HALO[level], k, u] = new

        rows_loop(lo, hi, body, unroll)

    def from_zero(dst, b, lo, hi, level):
        def body(r):
            m = mask(r, level)
            for k in range(2):
                c = m * (WEIGHT / (4.0 / 4.0**level + F[k]))
                for u in range(WIDTH[level]):
                    dst[r, k, u] = c * b[r, k, u]

        rows_loop(lo, hi, body)

    def residual(v, b, coarse, lo, count, at, level):
        h2 = 4.0**level
        wide = WIDTH[level]

        def body(i):
            total = [[zero] * wide for _ in range(2)]
            for j in range(2):
                r = lo + 2 * i + j
                mid, nb = around(v, r, level, load)
                for k in range(2):
                    for u in range(wide):
                        x = (
                            b[r, k, u]
                            + (nb[k][u] - 4.0 * mid[k][u]) * (1.0 / h2)
                            - F[k] * (mid[k][u] - mid[1 - k][u])
                        )
                        total[k][u] = x if j == 0 else total[k][u] + x
            for k in range(2):
                t = total[k]
                if level < 2:
                    for u in range(wide // 2):
                        coarse[at + i, k, u] = 0.25 * (t[2 * u] + t[2 * u + 1])
                else:
                    s = 1 if level == 2 else 2
                    odd = odd1 if level == 2 else odd2
                    other = jnp.where(odd, pltpu.roll(t[0], s, 0), pltpu.roll(t[0], 8 - s, 0))
                    coarse[at + i, k, 0] = 0.25 * (t[0] + other)

        rows_loop(0, count, body, 4 if level == 0 else 5)

    def prolong(v, coarse, lo, hi, level, shift):
        def body(r):
            i = (r + shift) // 2 if isinstance(r, int) else lax.div(r + shift, 2)
            for k in range(2):
                for u in range(WIDTH[level]):
                    cu = u // 2 if level < 2 else u
                    v[r, k, u] = v[r, k, u] + coarse[i, k, cu]

        rows_loop(lo, hi, body)

    def inside(d):
        return jnp.logical_and(me + d >= 0, me + d < n)

    copies = []

    def put(d, src, dst):
        copies.append((d, src, dst))
        return len(copies) - 1

    def copy(i, d, src, dst):
        return pltpu.make_async_remote_copy(
            src_ref=src,
            dst_ref=dst,
            send_sem=send.at[i],
            recv_sem=recv.at[i],
            device_id={"wide": me + d},
            device_id_type=MESH,
        )

    def start(ids):
        for i in ids:
            d, src, dst = copies[i]

            @pl.when(inside(d))
            def _():
                copy(i, d, src, dst).start()

    def arrive(ids):
        for i in ids:
            d, src, dst = copies[i]

            @pl.when(inside(-d))
            def _():
                copy(i, -d, src, dst).wait_recv()

    def depart(ids):
        for i in ids:
            d, src, dst = copies[i]

            @pl.when(inside(d))
            def _():
                copy(i, d, src, dst).wait_send()

    reach = min(REACH, n - 1)
    phase_a = [
        put(1, pq.at[pl.ds(17, 3)], pq.at[pl.ds(1, 3)]),
        put(-1, pq.at[pl.ds(4, 3)], pq.at[pl.ds(20, 3)]),
    ]
    phase_b = [
        put(1, b1.at[pl.ds(8, 4)], b1.at[pl.ds(0, 4)]),
        put(-1, b1.at[pl.ds(4, 4)], b1.at[pl.ds(12, 4)]),
    ]
    phase_c = [
        put(1, b2.at[pl.ds(5, 4)], b2.at[pl.ds(1, 4)]),
        put(-1, b2.at[pl.ds(5, 4)], b2.at[pl.ds(9, 4)]),
        put(2, b2.at[pl.ds(8, 1)], b2.at[pl.ds(0, 1)]),
        put(-2, b2.at[pl.ds(5, 1)], b2.at[pl.ds(13, 1)]),
    ]
    phase_e = [
        put(1, c0.at[pl.ds(18, 1)], c0.at[pl.ds(2, 1)]),
        put(-1, c0.at[pl.ds(5, 1)], c0.at[pl.ds(21, 1)]),
    ]
    phase_d = []
    for d in range(reach, 0, -1):
        for signed in (d, -d):
            phase_d.append(put(signed, g3.at[pl.ds(10, 1)], g3.at[pl.ds(10 - signed, 1)]))

    def clear(ref, lo, hi, inner):
        for r in range(lo, hi):
            for index in inner:
                ref[(r, *index)] = zero

    pairs = [(k, u) for k in range(2) for u in range(4)]

    @pl.when(me == 0)
    def _():
        clear(pq, 1, 4, [(f, k, u) for f in range(2) for k, u in pairs])
        clear(c0, 2, 3, pairs)

    @pl.when(me == n - 1)
    def _():
        clear(pq, 20, 23, [(f, k, u) for f in range(2) for k, u in pairs])
        clear(c0, 21, 22, pairs)

    clear(b1, 0, 4, [(k, u) for k in range(2) for u in range(2)])
    clear(b1, 12, 16, [(k, u) for k in range(2) for u in range(2)])
    clear(b2, 0, 5, [(0, 0), (1, 0)])
    clear(b2, 9, 14, [(0, 0), (1, 0)])
    clear(g3, 0, 10, [(0,), (1,)])
    clear(g3, 11, 21, [(0,), (1,)])

    barrier = pltpu.get_barrier_semaphore()
    for d in range(-reach, reach + 1):
        if d:

            @pl.when(inside(d))
            def _():
                pl.semaphore_signal(barrier, inc=1, device_id={"wide": me + d}, device_id_type=MESH)

    def take(j):
        def layer(k, carry):
            for f, ref in enumerate((p_in, q_in)):

                def load4(a):
                    return ref[k, pl.ds(4 * j, 4), pl.ds(128 * a, 128)]

                def store(q, u, x):
                    pq[4 + 4 * j + q, f, k, u] = x

                to_chunks(load4, store, xs.at[f], ts.at[f])
            return carry

        lax.fori_loop(0, 2, layer, 0)

    def give(ref, out, k, js):
        for j in js:

            def load1(q, u):
                return ref[4 * j + q, k, u]

            def store4(a, x):
                out[k, pl.ds(4 * j, 4), pl.ds(128 * a, 128)] = x

            from_chunks(load1, store4, xs.at[j % 2], ts.at[j % 2])

    take(0)
    take(3)
    pl.semaphore_wait(barrier, jnp.minimum(me, reach) + jnp.minimum(n - 1 - me, reach))
    start(phase_a)
    take(1)
    take(2)

    def advance(lo, hi, own):
        def body(r):
            for k in range(2):
                p = [[pq[r + j, 0, k, u] for u in range(4)] for j in (-1, 0, 1)]
                q = [[pq[r + j, 1, k, u] for u in range(4)] for j in (-1, 0, 1)]
                pe, pw = [east(x, 0) for x in p], [west(x, 0) for x in p]
                qe, qw = [east(x, 0) for x in q], [west(x, 0) for x in q]
                for u in range(4):
                    ps, pc, pn = (x[u] for x in p)
                    qs, qc, qnn = (x[u] for x in q)
                    pse, pce, pne = (x[u] for x in pe)
                    psw, pcw, pnw = (x[u] for x in pw)
                    qse, qce, qne = (x[u] for x in qe)
                    qsw, qcw, qnw = (x[u] for x in qw)
                    ns = qnn - qs
                    ew = qce - qcw
                    jac = (
                        pce * (ns + (qne - qse))
                        - pcw * (ns + (qnw - qsw))
                        - pn * (ew + (qne - qnw))
                        + ps * (ew + (qse - qsw))
                        + pne * (qnn - qce)
                        - pnw * (qnn - qcw)
                        - pse * (qs - qce)
                        + psw * (qs - qcw)
                    )
                    change = jac * (DT / 12.0) + (pce - pcw) * (DT * BETA * 0.5)
                    if k == 1:
                        change = change + (DT * DRAG) * ((pn + ps) + (pcw + pce) - 4.0 * pc)
                    b0[r, k, u] = change - qc
                    if own:
                        qn_ref[r - 4, k, u] = qc - change

        rows_loop(lo, hi, body, 2)

    advance(5, 19, True)
    arrive(phase_a)
    advance(2, 4, False)
    advance(4, 5, True)
    advance(19, 20, True)
    advance(20, 22, False)

    sweep(pq, a0, b0, 2, 22, 0, load_p, unroll=4)
    sweep(a0, c0, b0, 3, 21, 0, unroll=4)
    residual(c0, b0, b1, 4, 8, 4, 0)

    start(phase_b)
    start(phase_e)
    give(qn_ref, qn_out, 0, range(4))
    arrive(phase_b)
    from_zero(a1, b1, 0, 16, 1)
    sweep(a1, c1, b1, 1, 15, 1, unroll=7)
    residual(c1, b1, b2, 4, 4, 5, 1)

    start(phase_c)
    give(qn_ref, qn_out, 1, (0, 1))
    arrive(phase_c)
    from_zero(a2, b2, 0, 14, 2)
    sweep(a2, c2, b2, 1, 13, 2, unroll=12)
    residual(c2, b2, b3, 5, 2, 20, 2)

    for k in range(2):
        g3[10, k] = jnp.where(odd1, b3[21, k, 0], b3[20, k, 0])
    start(phase_d)
    give(qn_ref, qn_out, 1, (2, 3))
    arrive(phase_d)

    def unpack(i):
        for k in range(2):
            z = g3[i, k]
            b3[2 * i, k, 0] = jnp.where(odd1, pltpu.roll(z, 1, 0), z)
            b3[2 * i + 1, k, 0] = jnp.where(odd1, z, pltpu.roll(z, 7, 0))

    rows_loop(0, 21, unpack, 7)
    from_zero(a3, b3, 0, 42, 3)
    sweep(a3, c3, b3, 1, 41, 3, unroll=10)
    residual(c3, b3, b4, 2, 19, 0, 3)

    from_zero(a4, b4, 0, 19, 4)
    x, y = a4, c4
    for j in range(1, 8):
        sweep(x, y, b4, j, 19 - j, 4, unroll=20)
        x, y = y, x

    prolong(c3, x, 16, 26, 3, -2)
    sweep(c3, a3, b3, 17, 25, 3, unroll=8)
    sweep(a3, c3, b3, 18, 24, 3, unroll=8)

    prolong(c2, c3, 1, 13, 2, 35)
    sweep(c2, a2, b2, 2, 12, 2, unroll=12)
    sweep(a2, c2, b2, 3, 11, 2, unroll=12)

    prolong(c1, c2, 1, 15, 1, 6)
    sweep(c1, a1, b1, 2, 14, 1, unroll=6)
    sweep(a1, c1, b1, 3, 13, 1, unroll=5)

    arrive(phase_e)
    depart(phase_e)
    prolong(c0, c1, 2, 22, 0, 4)
    sweep(c0, a0, b0, 3, 21, 0, unroll=4)
    sweep(a0, sn_ref, b0, 4, 20, 0, out=True, unroll=4)

    for k in range(2):
        give(sn_ref, sn_out, k, range(4))
    depart(phase_a + phase_b + phase_c + phase_d)


def shards(stream_now, vorticity):
    n = lax.axis_size("wide")
    vmem = pl.BlockSpec(memory_space=pltpu.VMEM)
    shape = jax.ShapeDtypeStruct((2, ROWS, 4096), jnp.float32)
    scratch = [pltpu.VMEM((2, 128, 128), jnp.float32)] * 2
    scratch += [pltpu.VMEM((ROWS, 2, 4, 8, 128), jnp.float32)] * 2
    scratch += [pltpu.VMEM((EXT[0], 2, 2, 4, 8, 128), jnp.float32)]
    for level in range(5):
        scratch += [pltpu.VMEM((EXT[level], 2, WIDTH[level], 8, 128), jnp.float32)] * 3
    count = 10 + 2 * min(REACH, n - 1)
    return pl.pallas_call(
        functools.partial(kernel, n),
        out_shape=(shape, shape),
        in_specs=[vmem, vmem],
        out_specs=(vmem, vmem),
        scratch_shapes=scratch
        + [pltpu.VMEM((2 * REACH + 1, 2, 8, 128), jnp.float32)]
        + [pltpu.SemaphoreType.DMA((count,)), pltpu.SemaphoreType.DMA((count,))],
        compiler_params=pltpu.CompilerParams(
            collective_id=0, has_side_effects=True, vmem_limit_bytes=40 * 1024 * 1024
        ),
    )(stream_now, vorticity)


def solution(mesh):
    return jax.shard_map(
        shards,
        mesh=mesh,
        in_specs=(P("member", "wide", None), P("member", "wide", None)),
        out_specs=(P("member", "wide", None), P("member", "wide", None)),
        check_vma=False,
    )
```

```python
import functools

import jax
import jax.numpy as jnp
from jax import lax
from jax.experimental import pallas as pl
from jax.experimental.pallas import tpu as pltpu
from jax.sharding import PartitionSpec as P

MESH = pl.DeviceIdType.MESH
WEIGHT = 0.8
F = (0.02, 0.04)
DT = 0.5
BETA = 0.05
DRAG = 0.02

ROWS = 16
WIDTH = (4, 2, 1, 1, 1)
STEP = (1, 1, 1, 2, 4)
HALO = (4, 4, 5, 20, 9)
OWN = (16, 8, 4, 2, 1)
EXT = tuple(o + 2 * h for o, h in zip(OWN, HALO))
REACH = 10


def rows_loop(lo, hi, body, unroll=4):
    count = hi - lo
    if count <= unroll:
        for r in range(lo, hi):
            body(r)
        return
    trips = count // unroll

    def trip(i, carry):
        for j in range(unroll):
            body(lo + i * unroll + j)
        return carry

    lax.fori_loop(0, trips, trip, 0)
    for r in range(lo + trips * unroll, hi):
        body(r)


def to_chunks(load4, store, xs, ts):
    for a in range(32):
        xs[pl.ds(4 * a, 4), :] = load4(a)
    ts[...] = xs[...].T
    lane = lax.broadcasted_iota(jnp.int32, (8, 128), 1) & 3
    for u in range(4):
        part = [ts[pl.ds(32 * c + u, 8, stride=4), :] for c in range(4)]
        for q in range(4):
            out = part[q]
            for c in range(4):
                if c != q:
                    out = jnp.where(lane == c, pltpu.roll(part[c], (c - q) % 128, 1), out)
            store(q, u, out)


def from_chunks(load, store4, xs, ts):
    lane = lax.broadcasted_iota(jnp.int32, (8, 128), 1) & 3
    for u in range(4):
        part = [load(q, u) for q in range(4)]
        for c in range(4):
            out = part[c]
            for q in range(4):
                if q != c:
                    out = jnp.where(lane == q, pltpu.roll(part[q], (q - c) % 128, 1), out)
            ts[pl.ds(32 * c + u, 8, stride=4), :] = out
    xs[...] = ts[...].T
    for a in range(32):
        store4(a, xs[pl.ds(4 * a, 4), :])


def kernel(n, p_hbm, q_hbm, qn_out, sn_out, xs, ts, qn_ref, sn_ref, pq, b0, a0, c0, b1, a1, c1, b2, a2, c2, b3, a3, c3, b4, a4, c4, g3, p_in, q_in, fetch, send, recv):
    fetches = [
        pltpu.make_async_copy(p_hbm, p_in, fetch.at[0]),
        pltpu.make_async_copy(q_hbm, q_in, fetch.at[1]),
    ]
    for f in fetches:
        f.start()
    me = lax.axis_index("wide")
    sub = lax.broadcasted_iota(jnp.int32, (8, 128), 0)
    first = [sub < s for s in (1, 1, 1, 2, 4)]
    last = [sub >= 8 - s for s in (1, 1, 1, 2, 4)]
    odd1 = (sub & 1) != 0
    odd2 = (sub & 2) != 0
    zero = jnp.zeros((8, 128), jnp.float32)

    def east(v, level):
        s = STEP[level]
        z = pltpu.roll(v[0], 8 - s, 0)
        return v[1:] + [jnp.where(last[level], pltpu.roll(z, 127, 1), z)]

    def west(v, level):
        s = STEP[level]
        z = pltpu.roll(v[-1], s, 0)
        return [jnp.where(first[level], pltpu.roll(z, 1, 1), z)] + v[:-1]

    def mask(r, level):
        g = me * OWN[level] + r - HALO[level]
        return jnp.where(jnp.logical_and(g >= 0, g < n * OWN[level]), 1.0, 0.0).astype(jnp.float32)

    def load(ref, r, level):
        return [[ref[r, k, u] for u in range(WIDTH[level])] for k in range(2)]

    def load_p(ref, r, level):
        return [[ref[r, 0, k, u] for u in range(4)] for k in range(2)]

    def around(src, r, level, get):
        up, mid, down = get(src, r + 1, level), get(src, r, level), get(src, r - 1, level)
        nb = []
        for k in range(2):
            e, w = east(mid[k], level), west(mid[k], level)
            nb.append([up[k][u] + down[k][u] + (e[u] + w[u]) for u in range(WIDTH[level])])
        return mid, nb

    def sweep(src, dst, b, lo, hi, level, get=load, out=None, unroll=4):
        h2 = 4.0**level

        def body(r):
            m = mask(r, level)
            mid, nb = around(src, r, level, get)
            for k in range(2):
                c = m * (WEIGHT / (4.0 / h2 + F[k]))
                keep = m * (1.0 - WEIGHT)
                for u in range(WIDTH[level]):
                    new = keep * mid[k][u] + c * (
                        b[r, k, u] + nb[k][u] * (1.0 / h2) + F[k] * mid[1 - k][u]
                    )
                    if out is None:
                        dst[r, k, u] = new
                    else:
                        dst[r - HALO[level], k, u] = new

        rows_loop(lo, hi, body, unroll)

    def from_zero(dst, b, lo, hi, level):
        def body(r):
            m = mask(r, level)
            for k in range(2):
                c = m * (WEIGHT / (4.0 / 4.0**level + F[k]))
                for u in range(WIDTH[level]):
                    dst[r, k, u] = c * b[r, k, u]

        rows_loop(lo, hi, body)

    def residual(v, b, coarse, lo, count, at, level):
        h2 = 4.0**level
        wide = WIDTH[level]

        def body(i):
            total = [[zero] * wide for _ in range(2)]
            for j in range(2):
                r = lo + 2 * i + j
                mid, nb = around(v, r, level, load)
                for k in range(2):
                    for u in range(wide):
                        x = (
                            b[r, k, u]
                            + (nb[k][u] - 4.0 * mid[k][u]) * (1.0 / h2)
                            - F[k] * (mid[k][u] - mid[1 - k][u])
                        )
                        total[k][u] = x if j == 0 else total[k][u] + x
            for k in range(2):
                t = total[k]
                if level < 2:
                    for u in range(wide // 2):
                        coarse[at + i, k, u] = 0.25 * (t[2 * u] + t[2 * u + 1])
                else:
                    s = 1 if level == 2 else 2
                    odd = odd1 if level == 2 else odd2
                    other = jnp.where(odd, pltpu.roll(t[0], s, 0), pltpu.roll(t[0], 8 - s, 0))
                    coarse[at + i, k, 0] = 0.25 * (t[0] + other)

        rows_loop(0, count, body, 4 if level == 0 else 5)

    def prolong(v, coarse, lo, hi, level, shift):
        def body(r):
            i = (r + shift) // 2 if isinstance(r, int) else lax.div(r + shift, 2)
            for k in range(2):
                for u in range(WIDTH[level]):
                    cu = u // 2 if level < 2 else u
                    v[r, k, u] = v[r, k, u] + coarse[i, k, cu]

        rows_loop(lo, hi, body)

    def inside(d):
        return jnp.logical_and(me + d >= 0, me + d < n)

    copies = []

    def put(d, src, dst):
        copies.append((d, src, dst))
        return len(copies) - 1

    def copy(i, d, src, dst):
        return pltpu.make_async_remote_copy(
            src_ref=src,
            dst_ref=dst,
            send_sem=send.at[i],
            recv_sem=recv.at[i],
            device_id={"wide": me + d},
            device_id_type=MESH,
        )

    def start(ids):
        for i in ids:
            d, src, dst = copies[i]

            @pl.when(inside(d))
            def _():
                copy(i, d, src, dst).start()

    def arrive(ids):
        for i in ids:
            d, src, dst = copies[i]

            @pl.when(inside(-d))
            def _():
                copy(i, -d, src, dst).wait_recv()

    def depart(ids):
        for i in ids:
            d, src, dst = copies[i]

            @pl.when(inside(d))
            def _():
                copy(i, d, src, dst).wait_send()

    reach = min(REACH, n - 1)
    phase_a = [
        put(1, pq.at[pl.ds(17, 3)], pq.at[pl.ds(1, 3)]),
        put(-1, pq.at[pl.ds(4, 3)], pq.at[pl.ds(20, 3)]),
    ]
    phase_b = [
        put(1, b1.at[pl.ds(8, 4)], b1.at[pl.ds(0, 4)]),
        put(-1, b1.at[pl.ds(4, 4)], b1.at[pl.ds(12, 4)]),
    ]
    phase_c = [
        put(1, b2.at[pl.ds(5, 4)], b2.at[pl.ds(1, 4)]),
        put(-1, b2.at[pl.ds(5, 4)], b2.at[pl.ds(9, 4)]),
        put(2, b2.at[pl.ds(8, 1)], b2.at[pl.ds(0, 1)]),
        put(-2, b2.at[pl.ds(5, 1)], b2.at[pl.ds(13, 1)]),
    ]
    phase_e = [
        put(1, c0.at[pl.ds(18, 1)], c0.at[pl.ds(2, 1)]),
        put(-1, c0.at[pl.ds(5, 1)], c0.at[pl.ds(21, 1)]),
    ]
    phase_d = []
    for d in range(reach, 0, -1):
        for signed in (d, -d):
            phase_d.append(put(signed, g3.at[pl.ds(10, 1)], g3.at[pl.ds(10 - signed, 1)]))

    def clear(ref, lo, hi, inner):
        for r in range(lo, hi):
            for index in inner:
                ref[(r, *index)] = zero

    pairs = [(k, u) for k in range(2) for u in range(4)]

    @pl.when(me == 0)
    def _():
        clear(pq, 1, 4, [(f, k, u) for f in range(2) for k, u in pairs])
        clear(c0, 2, 3, pairs)

    @pl.when(me == n - 1)
    def _():
        clear(pq, 20, 23, [(f, k, u) for f in range(2) for k, u in pairs])
        clear(c0, 21, 22, pairs)

    clear(b1, 0, 4, [(k, u) for k in range(2) for u in range(2)])
    clear(b1, 12, 16, [(k, u) for k in range(2) for u in range(2)])
    clear(b2, 0, 5, [(0, 0), (1, 0)])
    clear(b2, 9, 14, [(0, 0), (1, 0)])
    clear(g3, 0, 10, [(0,), (1,)])
    clear(g3, 11, 21, [(0,), (1,)])

    barrier = pltpu.get_barrier_semaphore()
    for d in range(-reach, reach + 1):
        if d:

            @pl.when(inside(d))
            def _():
                pl.semaphore_signal(barrier, inc=1, device_id={"wide": me + d}, device_id_type=MESH)

    def take(j):
        def layer(k, carry):
            for f, ref in enumerate((p_in, q_in)):

                def load4(a):
                    return ref[k, pl.ds(4 * j, 4), pl.ds(128 * a, 128)]

                def store(q, u, x):
                    pq[4 + 4 * j + q, f, k, u] = x

                to_chunks(load4, store, xs.at[f], ts.at[f])
            return carry

        lax.fori_loop(0, 2, layer, 0)

    def give(ref, out, k, js):
        for j in js:

            def load1(q, u):
                return ref[4 * j + q, k, u]

            def store4(a, x):
                out[k, pl.ds(4 * j, 4), pl.ds(128 * a, 128)] = x

            from_chunks(load1, store4, xs.at[j % 2], ts.at[j % 2])

    for f in fetches:
        f.wait()
    take(0)
    take(3)
    pl.semaphore_wait(barrier, jnp.minimum(me, reach) + jnp.minimum(n - 1 - me, reach))
    start(phase_a)
    take(1)
    take(2)

    def advance(lo, hi, own):
        def body(r):
            for k in range(2):
                p = [[pq[r + j, 0, k, u] for u in range(4)] for j in (-1, 0, 1)]
                q = [[pq[r + j, 1, k, u] for u in range(4)] for j in (-1, 0, 1)]
                pe, pw = [east(x, 0) for x in p], [west(x, 0) for x in p]
                qe, qw = [east(x, 0) for x in q], [west(x, 0) for x in q]
                for u in range(4):
                    ps, pc, pn = (x[u] for x in p)
                    qs, qc, qnn = (x[u] for x in q)
                    pse, pce, pne = (x[u] for x in pe)
                    psw, pcw, pnw = (x[u] for x in pw)
                    qse, qce, qne = (x[u] for x in qe)
                    qsw, qcw, qnw = (x[u] for x in qw)
                    ns = qnn - qs
                    ew = qce - qcw
                    jac = (
                        pce * (ns + (qne - qse))
                        - pcw * (ns + (qnw - qsw))
                        - pn * (ew + (qne - qnw))
                        + ps * (ew + (qse - qsw))
                        + pne * (qnn - qce)
                        - pnw * (qnn - qcw)
                        - pse * (qs - qce)
                        + psw * (qs - qcw)
                    )
                    change = jac * (DT / 12.0) + (pce - pcw) * (DT * BETA * 0.5)
                    if k == 1:
                        change = change + (DT * DRAG) * ((pn + ps) + (pcw + pce) - 4.0 * pc)
                    b0[r, k, u] = change - qc
                    if own:
                        qn_ref[r - 4, k, u] = qc - change

        rows_loop(lo, hi, body, 2)

    advance(5, 19, True)
    arrive(phase_a)
    advance(2, 4, False)
    advance(4, 5, True)
    advance(19, 20, True)
    advance(20, 22, False)

    sweep(pq, a0, b0, 2, 22, 0, load_p, unroll=4)
    sweep(a0, c0, b0, 3, 21, 0, unroll=4)
    residual(c0, b0, b1, 4, 8, 4, 0)

    start(phase_b)
    start(phase_e)
    give(qn_ref, qn_out, 0, range(4))
    arrive(phase_b)
    from_zero(a1, b1, 0, 16, 1)
    sweep(a1, c1, b1, 1, 15, 1, unroll=7)
    residual(c1, b1, b2, 4, 4, 5, 1)

    start(phase_c)
    give(qn_ref, qn_out, 1, (0, 1))
    arrive(phase_c)
    from_zero(a2, b2, 0, 14, 2)
    sweep(a2, c2, b2, 1, 13, 2, unroll=12)
    residual(c2, b2, b3, 5, 2, 20, 2)

    for k in range(2):
        g3[10, k] = jnp.where(odd1, b3[21, k, 0], b3[20, k, 0])
    start(phase_d)
    give(qn_ref, qn_out, 1, (2, 3))
    arrive(phase_d)

    def unpack(i):
        for k in range(2):
            z = g3[i, k]
            b3[2 * i, k, 0] = jnp.where(odd1, pltpu.roll(z, 1, 0), z)
            b3[2 * i + 1, k, 0] = jnp.where(odd1, z, pltpu.roll(z, 7, 0))

    rows_loop(0, 21, unpack, 7)
    from_zero(a3, b3, 0, 42, 3)
    sweep(a3, c3, b3, 1, 41, 3, unroll=10)
    residual(c3, b3, b4, 2, 19, 0, 3)

    from_zero(a4, b4, 0, 19, 4)
    x, y = a4, c4
    for j in range(1, 8):
        sweep(x, y, b4, j, 19 - j, 4, unroll=20)
        x, y = y, x

    prolong(c3, x, 16, 26, 3, -2)
    sweep(c3, a3, b3, 17, 25, 3, unroll=8)
    sweep(a3, c3, b3, 18, 24, 3, unroll=8)

    prolong(c2, c3, 1, 13, 2, 35)
    sweep(c2, a2, b2, 2, 12, 2, unroll=12)
    sweep(a2, c2, b2, 3, 11, 2, unroll=12)

    prolong(c1, c2, 1, 15, 1, 6)
    sweep(c1, a1, b1, 2, 14, 1, unroll=6)
    sweep(a1, c1, b1, 3, 13, 1, unroll=5)

    arrive(phase_e)
    depart(phase_e)
    prolong(c0, c1, 2, 22, 0, 4)
    sweep(c0, a0, b0, 3, 21, 0, unroll=4)
    sweep(a0, sn_ref, b0, 4, 20, 0, out=True, unroll=4)

    for k in range(2):
        give(sn_ref, sn_out, k, range(4))
    depart(phase_a + phase_b + phase_c + phase_d)


def shards(stream_now, vorticity):
    n = lax.axis_size("wide")
    vmem = pl.BlockSpec(memory_space=pltpu.VMEM)
    shape = jax.ShapeDtypeStruct((2, ROWS, 4096), jnp.float32)
    scratch = [pltpu.VMEM((2, 128, 128), jnp.float32)] * 2
    scratch += [pltpu.VMEM((ROWS, 2, 4, 8, 128), jnp.float32)] * 2
    scratch += [pltpu.VMEM((EXT[0], 2, 2, 4, 8, 128), jnp.float32)]
    for level in range(5):
        scratch += [pltpu.VMEM((EXT[level], 2, WIDTH[level], 8, 128), jnp.float32)] * 3
    count = 10 + 2 * min(REACH, n - 1)
    return pl.pallas_call(
        functools.partial(kernel, n),
        out_shape=(shape, shape),
        in_specs=[pl.BlockSpec(memory_space=pltpu.HBM)] * 2,
        out_specs=(vmem, vmem),
        scratch_shapes=scratch
        + [pltpu.VMEM((2 * REACH + 1, 2, 8, 128), jnp.float32)]
        + [pltpu.VMEM((2, ROWS, 4096), jnp.float32)] * 2
        + [pltpu.SemaphoreType.DMA((2,))]
        + [pltpu.SemaphoreType.DMA((count,)), pltpu.SemaphoreType.DMA((count,))],
        compiler_params=pltpu.CompilerParams(
            collective_id=0, has_side_effects=True, vmem_limit_bytes=40 * 1024 * 1024
        ),
    )(stream_now, vorticity)


def solution(mesh):
    return jax.shard_map(
        shards,
        mesh=mesh,
        in_specs=(P("member", "wide", None), P("member", "wide", None)),
        out_specs=(P("member", "wide", None), P("member", "wide", None)),
        check_vma=False,
    )
```
